32 devices in a mesh: groups: 2 (over x), dp: 16 (over z, y, core).
Axes of the slice: x: 2, y: 2, z: 4, core: 2. Of those that a mesh axis runs over, the one named last changes fastest.
Arguments:
- train_acts: bfloat16 [8192, 8192], P(('groups', 'dp')), parts along dimension 0, may hold values from -6 to 6
- train_grads: bfloat16 [8192, 14336], P(('groups', 'dp')), parts along dimension 0
- lengths: int32 [64], P(('groups', 'dp')), parts along dimension 0, may hold values from 32 to 128
- query_in: bfloat16 [128, 8192], P('dp'), may hold values from -0.0625 to 0.0625
- query_out: bfloat16 [128, 14336], P('dp'), may hold values from -0.046875 to 0.046875
Outputs:
- influence: float32 [64, 4], P(('groups', 'dp')), parts along dimension 0
The draws below stay inside these ranges and needn't reach their ends.
There are 2 independent parts, one for each index of `groups`. The reference program is written for one: setup_inputs(seed, part) draws one part's arguments, and reference() takes and returns one part's arrays. A program takes and returns all parts, laid end to end along the dimension named above; an argument that names none is the same for every part. Nothing has to cross between parts.
All inputs are finite; a program needn't handle non-finite values.
Results may differ from the reference program's by a relative error of at most 0.0003.
Values may be sent and summed in bfloat16 or wider, within the bound.
A program may use at most 128 MiB of HBM per device.

```python
import math
import jax
import jax.numpy as jnp
from jax import lax

D = 8192
FFW = 14336
RANK = 32
LEN = 128
SEQ_DEV = 2
SEQUENCES = 32
TOKENS = 4096
ROWS_ALL = 128
QUERIES = 4
N_DP = 16


def draw_train_grads(key, part):
    key = jax.random.fold_in(key, 11)
    key_spread, key_noise = jax.random.split(key, 2)
    position = jnp.arange(SEQUENCES, dtype=jnp.float32) / max(SEQUENCES - 1, 1)
    rising = jnp.sqrt(1.0 + 2.0 * position)
    spread = jnp.exp(jax.random.uniform(key_spread, (SEQUENCES,), minval=0.0, maxval=math.log(10.0)))
    noise_field = jnp.clip(jax.random.normal(key_noise, (SEQUENCES * LEN, FFW)), -5.0, 5.0)
    scale = jnp.repeat(rising * spread, LEN)[:, None]
    return (noise_field * scale).astype(jnp.float32).astype(jnp.bfloat16)


def set_ends(values, key, smallest, high):
    longest = values.shape.index(max(values.shape))
    spots = []
    for shift in (0, 1):
        where = [jax.random.randint(jax.random.fold_in(key, axis), (), 0, length) for axis, length in enumerate(values.shape)]
        where[longest] = (where[longest] + shift) % values.shape[longest]
        spots.append(tuple(where))
    return values.at[spots[0]].set(smallest).at[spots[1]].set(high)


def levels(own_key, dims, shards, least, top_value):
    loudness, own = 1.0, jax.random.fold_in(own_key, 6)
    for dim, blocks in shards:
        steps = jnp.exp(jax.random.uniform(jax.random.fold_in(own, dim), (blocks,), jnp.float32, least / len(shards), top_value / len(shards)))
        loudness = loudness * jnp.repeat(steps, dims[dim] // blocks).reshape([-1 if axis == dim else 1 for axis in range(len(dims))])
    return loudness


def scatter_about(rng, shape, scale, bound, cuts=(), kind=jnp.bfloat16):
    values = scale * jax.random.normal(rng, shape, jnp.float32)
    if cuts:
        values = values * levels(rng, shape, cuts, -0.22, 0.18)
    return jnp.clip(values, -bound, bound).astype(kind)


def setup_inputs(seed: int = 0, part: int = 0) -> dict:
    key_of = jax.random.split(jax.random.key(seed), 6)
    part_splits = jax.random.split(jax.random.fold_in(key_of[5], part), 6)
    train_acts = scatter_about(part_splits[0], (TOKENS, D), 1.0, 6.0, ((0, 16),))
    train_grads = draw_train_grads(jax.random.fold_in(jax.random.fold_in(key_of[5], part), 71), part)
    lengths = set_ends(jax.random.randint(part_splits[2], (SEQUENCES,), LEN // 4, LEN + 1), jax.random.fold_in(part_splits[2], 1), LEN // 4, LEN).astype(jnp.int32)
    query_in = scatter_about(key_of[3], (ROWS_ALL, D), D ** -0.5, 0.0625, ((0, 16),))
    query_out = scatter_about(key_of[4], (ROWS_ALL, FFW), FFW ** -0.5, 0.046875, ((0, 16),))
    return dict(train_acts=train_acts, train_grads=train_grads, lengths=lengths, query_in=query_in, query_out=query_out)


def reference(train_acts, train_grads, lengths, query_in, query_out):
    query_left = query_in.astype(jnp.float32)
    query_right = query_out.astype(jnp.float32)
    owner_ids = jnp.arange(ROWS_ALL, dtype=jnp.int32) // RANK
    onehot = (owner_ids[None, :] == jnp.arange(QUERIES, dtype=jnp.int32)[:, None]).astype(jnp.float32)
    acts_blocks = train_acts.reshape(N_DP, SEQ_DEV * LEN, D)
    grads_blocks = train_grads.reshape(N_DP, SEQ_DEV * LEN, FFW)
    length_blocks = lengths.reshape(N_DP, SEQ_DEV)

    def score_block(block_item):
        acts_here, grads_here, lengths_here = block_item
        left_proj = jnp.dot(query_left, acts_here.astype(jnp.float32).T, precision=lax.Precision.HIGHEST)
        right_proj = jnp.dot(query_right, grads_here.astype(jnp.float32).T, precision=lax.Precision.HIGHEST)
        valid_mask = (jnp.arange(LEN, dtype=jnp.int32)[None, :] < lengths_here[:, None]).astype(jnp.float32)
        product = (left_proj * right_proj).reshape(ROWS_ALL, SEQ_DEV, LEN)
        row_score = lax.optimization_barrier(jnp.sum(product * valid_mask[None], axis=2))
        return jnp.dot(onehot, row_score, precision=lax.Precision.HIGHEST).T
    scores = lax.map(score_block, (acts_blocks, grads_blocks, length_blocks)).reshape(SEQUENCES, QUERIES)
    spread = lax.optimization_barrier(jnp.mean(scores * scores, axis=0))
    return scores / jnp.sqrt(spread + 1e-06)
```

```python
import functools

import jax
import jax.numpy as jnp
from jax import lax
from jax.experimental import pallas as pl
from jax.experimental.pallas import tpu as pltpu
from jax.sharding import PartitionSpec as P

RANK = 32
MESH = pl.DeviceIdType.MESH
WIDTH = 2048


def plain_body(train_acts, train_grads, lengths, query_in, query_out):
    token_rows = train_acts.shape[0]
    seq_count = lengths.shape[0]
    seq_len = token_rows // seq_count
    device_count = lax.axis_size("dp")
    total_rows = query_in.shape[0] * device_count
    query_count = total_rows // RANK
    valid_mask = (jnp.arange(seq_len, dtype=jnp.int32)[None, :] < lengths[:, None]).astype(
        jnp.float32
    )
    all_left, all_right = (
        lax.all_gather(query_in, "dp", axis=0, tiled=True),
        lax.all_gather(query_out, "dp", axis=0, tiled=True),
    )
    left_proj = lax.dot_general(
        all_left, train_acts, (((1,), (1,)), ((), ())), preferred_element_type=jnp.float32
    )
    right_proj = lax.dot_general(
        all_right, train_grads, (((1,), (1,)), ((), ())), preferred_element_type=jnp.float32
    )
    product = (left_proj * right_proj).reshape(all_left.shape[0], seq_count, seq_len)
    onehot = (
        (jnp.arange(total_rows, dtype=jnp.int32) // RANK)[None, :]
        == jnp.arange(query_count, dtype=jnp.int32)[:, None]
    ).astype(jnp.float32)
    scores = jnp.dot(
        onehot, jnp.sum(product * valid_mask[None], axis=2), precision=lax.Precision.HIGHEST
    )
    squares = lax.psum(jnp.sum(scores * scores, axis=1), "dp")
    spread = squares / (seq_count * device_count)
    return (scores / jnp.sqrt(spread + 1e-06)[:, None]).T


def make_plan(left_cols, right_cols):
    chunks = {"l": left_cols // WIDTH, "r": right_cols // WIDTH}
    total = chunks["l"] + chunks["r"]
    both = max(1, round(total * 3 / 11))
    if (total - both) % 2:
        both += 1
    plan = []
    for k in range(chunks["l"] // 2):
        plan.append(("pair", 0, 2 * k * WIDTH))
    pairs_right = (chunks["r"] - both) // 2
    for k in range(pairs_right):
        plan.append(("pair", 1, 2 * k * WIDTH))
    for k in range(2 * pairs_right, chunks["r"]):
        plan.append(("both", 1, k * WIDTH))
    return plan


def count_copies(plan):
    return sum(11 if kind == "pair" else 7 for kind, _, _ in plan)


def kernel(
    plan, seq_len, lengths_ref, acts_hbm, grads_hbm, qin_hbm, qout_hbm, out_ref,
    acts, grads, left, right, acc_left, acc_right, squares, local_sem, send_sem, recv_sem,
    sq_send, sq_recv,
):
    group = lax.axis_index("groups")
    me = lax.axis_index("dp")
    z, y, core = me // 4, (me // 2) % 2, me % 2

    def at(dz=0, dy=0, dc=0):
        return ((z + dz) % 4) * 4 + ((y + dy) % 2) * 2 + (core + dc) % 2

    z_peers = [(group, at(dz=d)) for d in (1, 2, 3)]
    y_peer = (group, at(dy=1))
    core_peer = (group, at(dc=1))
    x_peer = (1 - group, me)

    own_left = pltpu.make_async_copy(qin_hbm, left.at[0, 0, 0], local_sem.at[0])
    own_right = pltpu.make_async_copy(qout_hbm, right.at[0, 0, 0], local_sem.at[1])
    load_acts = pltpu.make_async_copy(acts_hbm, acts, local_sem.at[2])
    load_grads = pltpu.make_async_copy(grads_hbm, grads, local_sem.at[3])
    own_left.start()
    own_right.start()
    load_acts.start()
    load_grads.start()

    barrier = pltpu.get_barrier_semaphore()
    others = [(group, (me + d) % 16) for d in range(1, 16)]
    for other in others + [x_peer]:
        pl.semaphore_signal(barrier, inc=1, device_id=other, device_id_type=MESH)
    pl.semaphore_wait(barrier, 16)
    own_left.wait()
    own_right.wait()

    sides = (left, right)
    acc_left[...] = jnp.zeros_like(acc_left)
    acc_right[...] = jnp.zeros_like(acc_right)
    next_id = [0]
    sent = []

    def send(src, dst, peer):
        k = next_id[0]
        next_id[0] += 1
        copy = pltpu.make_async_remote_copy(
            src_ref=src, dst_ref=dst, send_sem=send_sem.at[k], recv_sem=recv_sem.at[k],
            device_id=peer, device_id_type=MESH,
        )
        return copy

    steps = []
    for kind, side, start in plan:
        buf = sides[side]
        step = dict(kind=kind, side=side, start=start)
        if kind == "pair":
            mine = pl.ds(pl.multiple_of(start + group * WIDTH, WIDTH), WIDTH)
            theirs = pl.ds(pl.multiple_of(start + (1 - group) * WIDTH, WIDTH), WIDTH)
        else:
            mine = pl.ds(start, WIDTH)
            theirs = None
        step["z"] = [
            send(buf.at[0, 0, 0, :, mine], buf.at[0, 0, 4 - d, :, mine], z_peers[d - 1])
            for d in (1, 2, 3)
        ]
        step["y0"] = send(buf.at[0, 0, 0, :, mine], buf.at[0, 1, 0, :, mine], y_peer)
        step["y"] = send(buf.at[0, 0, 1:4, :, mine], buf.at[0, 1, 1:4, :, mine], y_peer)
        step["c0"] = send(buf.at[0, 0, :, :, mine], buf.at[1, 0, :, :, mine], core_peer)
        step["c1"] = send(buf.at[0, 1, :, :, mine], buf.at[1, 1, :, :, mine], core_peer)
        if kind == "pair":
            step["x0"] = send(buf.at[0, 0, 1:4, :, mine], buf.at[0, 0, 1:4, :, mine], x_peer)
            step["x1"] = send(buf.at[0, 1, :, :, mine], buf.at[0, 1, :, :, mine], x_peer)
            step["x0r"] = buf.at[0, 0, 1:4, :, theirs]
            step["x1r"] = buf.at[0, 1, :, :, theirs]
            step["d0"] = send(buf.at[0, 0, :, :, theirs], buf.at[1, 0, :, :, theirs], core_peer)
            step["d1"] = send(buf.at[0, 1, :, :, theirs], buf.at[1, 1, :, :, theirs], core_peer)
        steps.append(step)

    def go(copy):
        copy.start()
        sent.append(copy)

    def bring(step):
        for copy in step["z"]:
            go(copy)
        go(step["y0"])

    def stage1(step):
        for copy in step["z"]:
            copy.wait_recv()
        go(step["y"])
        if step["kind"] == "pair":
            go(step["x0"])
        go(step["c0"])

    def stage2(step):
        step["y0"].wait_recv()
        step["y"].wait_recv()
        if step["kind"] == "pair":
            go(step["x1"])
        go(step["c1"])

    def stage3(step):
        if step["kind"] == "pair":
            step["x0"].wait_recv()
            go(step["d0"])
            step["x1"].wait_recv()
            go(step["d1"])

    loaded = [False, False]

    def stage4(step):
        step["c0"].wait_recv()
        step["c1"].wait_recv()
        if step["kind"] == "pair":
            step["d0"].wait_recv()
            step["d1"].wait_recv()
        side, start = step["side"], step["start"]
        if not loaded[side]:
            (load_acts, load_grads)[side].wait()
            loaded[side] = True
        width = WIDTH * (2 if step["kind"] == "pair" else 1)
        rows = sides[side][:, :, :, :, start:start + width].reshape(128, width)
        tokens = (acts, grads)[side][:, start:start + width]
        acc = (acc_left, acc_right)[side]
        acc[...] += lax.dot_general(
            rows, tokens, (((1,), (1,)), ((), ())), preferred_element_type=jnp.float32
        )

    for step in steps:
        bring(step)
    stages = (stage1, stage2, stage3, stage4)
    for i in range(len(steps) + 3):
        for lag, stage in enumerate(stages):
            if 0 <= i - lag < len(steps):
                stage(steps[i - lag])

    product = acc_left[...] * acc_right[...]
    tokens = product.shape[1]
    product = product.reshape(4, 4, 8, tokens)
    by_query = product[0] + product[1] + product[2] + product[3]
    row = lax.broadcasted_iota(jnp.int32, (8, 128), 0)
    lane = lax.broadcasted_iota(jnp.int32, (8, 128), 1)
    scores = jnp.zeros((8, 128), jnp.float32)
    for n in range(2):
        valid = lax.broadcasted_iota(jnp.int32, (8, seq_len), 1) < lengths_ref[n]
        for d in range(4):
            part = jnp.where(valid, by_query[d, :, n * seq_len:(n + 1) * seq_len], 0.0)
            total = jnp.sum(jnp.sum(part, axis=0, keepdims=True), axis=1, keepdims=True)
            scores += jnp.where((row == n) & (lane == (z + d) % 4), total, 0.0)

    squares[0] = scores * scores
    spreads = []
    for d in range(1, 16):
        copy = pltpu.make_async_remote_copy(
            src_ref=squares.at[0], dst_ref=squares.at[d], send_sem=sq_send.at[d - 1],
            recv_sem=sq_recv.at[d - 1], device_id=others[d - 1], device_id_type=MESH,
        )
        copy.start()
        spreads.append(copy)
    for copy in sent:
        copy.wait_send()
    for copy in spreads:
        copy.wait_recv()
    total = jnp.sum(jnp.sum(squares[...], axis=0), axis=0, keepdims=True)
    spread = total / 32.0
    out_ref[...] = scores / jnp.sqrt(spread + 1e-06)
    for copy in spreads:
        copy.wait_send()


def kernel_body(train_acts, train_grads, lengths, query_in, query_out):
    tokens, left_cols = train_acts.shape
    right_cols = train_grads.shape[1]
    seq_len = tokens // lengths.shape[0]
    plan = make_plan(left_cols, right_cols)
    copies = count_copies(plan)
    anywhere = pl.BlockSpec(memory_space=pl.ANY)
    tile = pl.pallas_call(
        functools.partial(kernel, plan, seq_len),
        out_shape=jax.ShapeDtypeStruct((8, 128), jnp.float32),
        in_specs=[pl.BlockSpec(memory_space=pltpu.SMEM)] + [anywhere] * 4,
        out_specs=pl.BlockSpec(memory_space=pltpu.VMEM),
        scratch_shapes=[
            pltpu.VMEM((tokens, left_cols), jnp.bfloat16),
            pltpu.VMEM((tokens, right_cols), jnp.bfloat16),
            pltpu.VMEM((2, 2, 4, 8, left_cols), jnp.bfloat16),
            pltpu.VMEM((2, 2, 4, 8, right_cols), jnp.bfloat16),
            pltpu.VMEM((128, tokens), jnp.float32),
            pltpu.VMEM((128, tokens), jnp.float32),
            pltpu.VMEM((16, 8, 128), jnp.float32),
            pltpu.SemaphoreType.DMA((4,)),
            pltpu.SemaphoreType.DMA((copies,)),
            pltpu.SemaphoreType.DMA((copies,)),
            pltpu.SemaphoreType.DMA((15,)),
            pltpu.SemaphoreType.DMA((15,)),
        ],
        compiler_params=pltpu.CompilerParams(
            collective_id=0, has_side_effects=True, vmem_limit_bytes=56 * 2**20
        ),
        cost_estimate=pl.CostEstimate(
            flops=2 * 128 * tokens * (left_cols + right_cols),
            bytes_accessed=2 * tokens * (left_cols + right_cols),
            transcendentals=0,
        ),
    )(lengths, train_acts, train_grads, query_in, query_out)
    return tile[:2, :4]


def solution(mesh):
    in_specs = (
        P(("groups", "dp"), None),
        P(("groups", "dp"), None),
        P(("groups", "dp")),
        P("dp", None),
        P("dp", None),
    )
    out_specs = P(("groups", "dp"), None)
    here = mesh.shape["groups"] == 2 and mesh.shape["dp"] == 16
    return jax.shard_map(
        kernel_body if here else plain_body,
        mesh=mesh, in_specs=in_specs, out_specs=out_specs, check_vma=False,
    )
```

```python
import functools

import jax
import jax.numpy as jnp
from jax import lax
from jax.experimental import pallas as pl
from jax.experimental.pallas import tpu as pltpu
from jax.sharding import PartitionSpec as P

RANK = 32
MESH = pl.DeviceIdType.MESH
WIDTH = 2048
AHEAD = 2
LATENCY = 3.0


def plain_body(train_acts, train_grads, lengths, query_in, query_out):
    token_rows = train_acts.shape[0]
    seq_count = lengths.shape[0]
    seq_len = token_rows // seq_count
    device_count = lax.axis_size("dp")
    total_rows = query_in.shape[0] * device_count
    query_count = total_rows // RANK
    valid_mask = (jnp.arange(seq_len, dtype=jnp.int32)[None, :] < lengths[:, None]).astype(
        jnp.float32
    )
    all_left, all_right = (
        lax.all_gather(query_in, "dp", axis=0, tiled=True),
        lax.all_gather(query_out, "dp", axis=0, tiled=True),
    )
    left_proj = lax.dot_general(
        all_left, train_acts, (((1,), (1,)), ((), ())), preferred_element_type=jnp.float32
    )
    right_proj = lax.dot_general(
        all_right, train_grads, (((1,), (1,)), ((), ())), preferred_element_type=jnp.float32
    )
    product = (left_proj * right_proj).reshape(all_left.shape[0], seq_count, seq_len)
    onehot = (
        (jnp.arange(total_rows, dtype=jnp.int32) // RANK)[None, :]
        == jnp.arange(query_count, dtype=jnp.int32)[:, None]
    ).astype(jnp.float32)
    scores = jnp.dot(
        onehot, jnp.sum(product * valid_mask[None], axis=2), precision=lax.Precision.HIGHEST
    )
    squares = lax.psum(jnp.sum(scores * scores, axis=1), "dp")
    spread = squares / (seq_count * device_count)
    return (scores / jnp.sqrt(spread + 1e-06)[:, None]).T


def make_plan(left_cols, right_cols):
    chunks = {"l": left_cols // WIDTH, "r": right_cols // WIDTH}
    total = chunks["l"] + chunks["r"]
    both = max(1, round(total * 3 / 11))
    if (total - both) % 2:
        both += 1
    plan = []
    for k in range(chunks["l"] // 2):
        plan.append(("pair", 0, 2 * k * WIDTH))
    pairs_right = (chunks["r"] - both) // 2
    for k in range(pairs_right):
        plan.append(("pair", 1, 2 * k * WIDTH))
    for k in range(2 * pairs_right, chunks["r"]):
        plan.append(("both", 1, k * WIDTH))
    return plan


def make_order(plan):
    events, asks = [], []
    z_free = y_free = x_free = 0.0
    ready = []
    for i, (kind, _, _) in enumerate(plan):
        z_free += 4.0
        z_in = z_free + LATENCY
        y_free = max(y_free, z_in) + (3.0 if i < AHEAD else 4.0)
        y_in = y_free + LATENCY
        events += [(z_in, i, "z"), (y_in, i, "y")]
        ready.append(y_in)
        if kind == "pair":
            asks += [(z_in, i, "x0", 3.0), (y_in, i, "x1", 4.0)]
    for time, i, name, blocks in sorted(asks):
        x_free = max(x_free, time) + blocks
        events.append((x_free + LATENCY, i, name))
        ready[i] = max(ready[i], x_free + LATENCY)
    for i, time in enumerate(ready):
        events.append((time + LATENCY, i, "done"))
    return sorted(events)


def count_copies(plan):
    return sum(11 if kind == "pair" else 7 for kind, _, _ in plan)


def kernel(
    plan, seq_len, lengths_ref, acts_hbm, grads_hbm, qin_hbm, qout_hbm, out_ref,
    acts, grads, left, right, acc_left, acc_right, squares, local_sem, send_sem, recv_sem,
    sq_send, sq_recv,
):
    group = lax.axis_index("groups")
    me = lax.axis_index("dp")
    z, y, core = me // 4, (me // 2) % 2, me % 2

    def at(dz=0, dy=0, dc=0):
        return ((z + dz) % 4) * 4 + ((y + dy) % 2) * 2 + (core + dc) % 2

    z_peers = [(group, at(dz=d)) for d in (1, 2, 3)]
    y_peer = (group, at(dy=1))
    core_peer = (group, at(dc=1))
    x_peer = (1 - group, me)

    own_left = pltpu.make_async_copy(qin_hbm, left.at[0, 0, 0], local_sem.at[0])
    own_right = pltpu.make_async_copy(qout_hbm, right.at[0, 0, 0], local_sem.at[1])
    load_acts = pltpu.make_async_copy(acts_hbm, acts, local_sem.at[2])
    load_grads = pltpu.make_async_copy(grads_hbm, grads, local_sem.at[3])
    own_left.start()
    own_right.start()
    load_acts.start()
    load_grads.start()

    barrier = pltpu.get_barrier_semaphore()
    others = [(group, (me + d) % 16) for d in range(1, 16)]
    for other in others + [x_peer]:
        pl.semaphore_signal(barrier, inc=1, device_id=other, device_id_type=MESH)
    pl.semaphore_wait(barrier, 16)
    own_left.wait()
    own_right.wait()

    sides = (left, right)
    acc_left[...] = jnp.zeros_like(acc_left)
    acc_right[...] = jnp.zeros_like(acc_right)
    next_id = [0]
    sent = []

    def send(src, dst, peer):
        k = next_id[0]
        next_id[0] += 1
        copy = pltpu.make_async_remote_copy(
            src_ref=src, dst_ref=dst, send_sem=send_sem.at[k], recv_sem=recv_sem.at[k],
            device_id=peer, device_id_type=MESH,
        )
        return copy

    steps = []
    for kind, side, start in plan:
        buf = sides[side]
        step = dict(kind=kind, side=side, start=start)
        if kind == "pair":
            mine = pl.ds(pl.multiple_of(start + group * WIDTH, WIDTH), WIDTH)
            theirs = pl.ds(pl.multiple_of(start + (1 - group) * WIDTH, WIDTH), WIDTH)
        else:
            mine = pl.ds(start, WIDTH)
            theirs = None
        step["z"] = [
            send(buf.at[0, 0, 0, :, mine], buf.at[0, 0, 4 - d, :, mine], z_peers[d - 1])
            for d in (1, 2, 3)
        ]
        step["y0"] = send(buf.at[0, 0, 0, :, mine], buf.at[0, 1, 0, :, mine], y_peer)
        step["y"] = send(buf.at[0, 0, 1:4, :, mine], buf.at[0, 1, 1:4, :, mine], y_peer)
        step["c0"] = send(buf.at[0, 0, :, :, mine], buf.at[1, 0, :, :, mine], core_peer)
        step["c1"] = send(buf.at[0, 1, :, :, mine], buf.at[1, 1, :, :, mine], core_peer)
        if kind == "pair":
            step["x0"] = send(buf.at[0, 0, 1:4, :, mine], buf.at[0, 0, 1:4, :, mine], x_peer)
            step["x1"] = send(buf.at[0, 1, :, :, mine], buf.at[0, 1, :, :, mine], x_peer)
            step["x0r"] = buf.at[0, 0, 1:4, :, theirs]
            step["x1r"] = buf.at[0, 1, :, :, theirs]
            step["d0"] = send(buf.at[0, 0, :, :, theirs], buf.at[1, 0, :, :, theirs], core_peer)
            step["d1"] = send(buf.at[0, 1, :, :, theirs], buf.at[1, 1, :, :, theirs], core_peer)
        steps.append(step)

    def go(copy):
        copy.start()
        sent.append(copy)

    def bring(step):
        for copy in step["z"]:
            go(copy)
        go(step["y0"])

    def stage1(step):
        for copy in step["z"]:
            copy.wait_recv()
        go(step["y"])
        if step["kind"] == "pair":
            go(step["x0"])
        go(step["c0"])

    def stage2(step):
        step["y0"].wait_recv()
        step["y"].wait_recv()
        if step["kind"] == "pair":
            go(step["x1"])
        go(step["c1"])

    def stage3a(step):
        step["x0"].wait_recv()
        go(step["d0"])

    def stage3b(step):
        step["x1"].wait_recv()
        go(step["d1"])

    loaded = [False, False]

    def stage4(step):
        step["c0"].wait_recv()
        step["c1"].wait_recv()
        if step["kind"] == "pair":
            step["d0"].wait_recv()
            step["d1"].wait_recv()
        side, start = step["side"], step["start"]
        if not loaded[side]:
            (load_acts, load_grads)[side].wait()
            loaded[side] = True
        width = WIDTH * (2 if step["kind"] == "pair" else 1)
        rows = sides[side][:, :, :, :, start:start + width].reshape(128, width)
        tokens = (acts, grads)[side][:, start:start + width]
        acc = (acc_left, acc_right)[side]
        acc[...] += lax.dot_general(
            rows, tokens, (((1,), (1,)), ((), ())), preferred_element_type=jnp.float32
        )

    for step in steps[:AHEAD]:
        bring(step)
    brought = AHEAD
    stages = dict(z=stage1, y=stage2, x0=stage3a, x1=stage3b, done=stage4)
    for _, i, name in make_order(plan):
        stages[name](steps[i])
        if name == "z" and brought < len(steps):
            bring(steps[brought])
            brought += 1

    product = acc_left[...] * acc_right[...]
    tokens = product.shape[1]
    product = product.reshape(4, 4, 8, tokens)
    by_query = product[0] + product[1] + product[2] + product[3]
    row = lax.broadcasted_iota(jnp.int32, (8, 128), 0)
    lane = lax.broadcasted_iota(jnp.int32, (8, 128), 1)
    scores = jnp.zeros((8, 128), jnp.float32)
    for n in range(2):
        valid = lax.broadcasted_iota(jnp.int32, (8, seq_len), 1) < lengths_ref[n]
        for d in range(4):
            part = jnp.where(valid, by_query[d, :, n * seq_len:(n + 1) * seq_len], 0.0)
            total = jnp.sum(jnp.sum(part, axis=0, keepdims=True), axis=1, keepdims=True)
            scores += jnp.where((row == n) & (lane == (z + d) % 4), total, 0.0)

    squares[0] = scores * scores
    spreads = []
    for d in range(1, 16):
        copy = pltpu.make_async_remote_copy(
            src_ref=squares.at[0], dst_ref=squares.at[d], send_sem=sq_send.at[d - 1],
            recv_sem=sq_recv.at[d - 1], device_id=others[d - 1], device_id_type=MESH,
        )
        copy.start()
        spreads.append(copy)
    for copy in sent:
        copy.wait_send()
    for copy in spreads:
        copy.wait_recv()
    total = jnp.sum(jnp.sum(squares[...], axis=0), axis=0, keepdims=True)
    spread = total / 32.0
    out_ref[...] = scores / jnp.sqrt(spread + 1e-06)
    for copy in spreads:
        copy.wait_send()


def kernel_body(train_acts, train_grads, lengths, query_in, query_out):
    tokens, left_cols = train_acts.shape
    right_cols = train_grads.shape[1]
    seq_len = tokens // lengths.shape[0]
    plan = make_plan(left_cols, right_cols)
    copies = count_copies(plan)
    anywhere = pl.BlockSpec(memory_space=pl.ANY)
    tile = pl.pallas_call(
        functools.partial(kernel, plan, seq_len),
        out_shape=jax.ShapeDtypeStruct((8, 128), jnp.float32),
        in_specs=[pl.BlockSpec(memory_space=pltpu.SMEM)] + [anywhere] * 4,
        out_specs=pl.BlockSpec(memory_space=pltpu.VMEM),
        scratch_shapes=[
            pltpu.VMEM((tokens, left_cols), jnp.bfloat16),
            pltpu.VMEM((tokens, right_cols), jnp.bfloat16),
            pltpu.VMEM((2, 2, 4, 8, left_cols), jnp.bfloat16),
            pltpu.VMEM((2, 2, 4, 8, right_cols), jnp.bfloat16),
            pltpu.VMEM((128, tokens), jnp.float32),
            pltpu.VMEM((128, tokens), jnp.float32),
            pltpu.VMEM((16, 8, 128), jnp.float32),
            pltpu.SemaphoreType.DMA((4,)),
            pltpu.SemaphoreType.DMA((copies,)),
            pltpu.SemaphoreType.DMA((copies,)),
            pltpu.SemaphoreType.DMA((15,)),
            pltpu.SemaphoreType.DMA((15,)),
        ],
        compiler_params=pltpu.CompilerParams(
            collective_id=0, has_side_effects=True, vmem_limit_bytes=56 * 2**20
        ),
        cost_estimate=pl.CostEstimate(
            flops=2 * 128 * tokens * (left_cols + right_cols),
            bytes_accessed=2 * tokens * (left_cols + right_cols),
            transcendentals=0,
        ),
    )(lengths, train_acts, train_grads, query_in, query_out)
    return tile[:2, :4]


def solution(mesh):
    in_specs = (
        P(("groups", "dp"), None),
        P(("groups", "dp"), None),
        P(("groups", "dp")),
        P("dp", None),
        P("dp", None),
    )
    out_specs = P(("groups", "dp"), None)
    here = mesh.shape["groups"] == 2 and mesh.shape["dp"] == 16
    return jax.shard_map(
        kernel_body if here else plain_body,
        mesh=mesh, in_specs=in_specs, out_specs=out_specs, check_vma=False,
    )
```

```python
import functools

import jax
import jax.numpy as jnp
from jax import lax
from jax.experimental import pallas as pl
from jax.experimental.pallas import tpu as pltpu
from jax.sharding import PartitionSpec as P

RANK = 32
MESH = pl.DeviceIdType.MESH
LEFT_PAIRS = (2048, 2048)
RIGHT_PAIRS = (2048, 1024)
BOTH = (2048, 2048, 2048, 2048)
AHEAD = 2
LATENCY = 3.0


def plain_body(train_acts, train_grads, lengths, query_in, query_out):
    token_rows = train_acts.shape[0]
    seq_count = lengths.shape[0]
    seq_len = token_rows // seq_count
    device_count = lax.axis_size("dp")
    total_rows = query_in.shape[0] * device_count
    query_count = total_rows // RANK
    valid_mask = (jnp.arange(seq_len, dtype=jnp.int32)[None, :] < lengths[:, None]).astype(
        jnp.float32
    )
    all_left, all_right = (
        lax.all_gather(query_in, "dp", axis=0, tiled=True),
        lax.all_gather(query_out, "dp", axis=0, tiled=True),
    )
    left_proj = lax.dot_general(
        all_left, train_acts, (((1,), (1,)), ((), ())), preferred_element_type=jnp.float32
    )
    right_proj = lax.dot_general(
        all_right, train_grads, (((1,), (1,)), ((), ())), preferred_element_type=jnp.float32
    )
    product = (left_proj * right_proj).reshape(all_left.shape[0], seq_count, seq_len)
    onehot = (
        (jnp.arange(total_rows, dtype=jnp.int32) // RANK)[None, :]
        == jnp.arange(query_count, dtype=jnp.int32)[:, None]
    ).astype(jnp.float32)
    scores = jnp.dot(
        onehot, jnp.sum(product * valid_mask[None], axis=2), precision=lax.Precision.HIGHEST
    )
    squares = lax.psum(jnp.sum(scores * scores, axis=1), "dp")
    spread = squares / (seq_count * device_count)
    return (scores / jnp.sqrt(spread + 1e-06)[:, None]).T


def make_plan(left_cols, right_cols):
    plan = []

    def add(kind, side, start, count, widths):
        for k in range(len(widths)):
            width = widths[k]
            plan.append((kind, side, start, width))
            start += width * (2 if kind == "pair" else 1)
            count -= width * (2 if kind == "pair" else 1)
        assert count == 0
        return start

    add("pair", 0, 0, left_cols, LEFT_PAIRS)
    start = add("pair", 1, 0, 2 * sum(RIGHT_PAIRS), RIGHT_PAIRS)
    add("both", 1, start, right_cols - start, BOTH)
    return plan


def make_order(plan):
    events, asks = [], []
    z_free = y_free = x_free = 0.0
    ready = []
    for i, (kind, _, _, width) in enumerate(plan):
        block = width / 2048
        z_free += 4.0 * block
        z_in = z_free + LATENCY
        y_free = max(y_free, z_in) + 3.0 * block
        y_in = y_free + LATENCY
        events += [(z_in, i, "z"), (y_in, i, "y")]
        ready.append(y_in)
        if kind == "pair":
            asks += [(z_in, i, "x0", 3.0 * block), (y_in, i, "x1", 4.0 * block)]
    for time, i, name, blocks in sorted(asks):
        x_free = max(x_free, time) + blocks
        events.append((x_free + LATENCY, i, name))
        ready[i] = max(ready[i], x_free + LATENCY)
    for i, time in enumerate(ready):
        events.append((time + LATENCY, i, "done"))
    return sorted(events)


def count_copies(plan):
    return sum(11 if step[0] == "pair" else 7 for step in plan)


def kernel(
    plan, seq_len, lengths_ref, acts_hbm, grads_hbm, qin_hbm, qout_hbm, out_ref,
    acts, grads, left, right, acc_left, acc_right, squares, local_sem, send_sem, recv_sem,
    sq_send, sq_recv,
):
    group = lax.axis_index("groups")
    me = lax.axis_index("dp")
    z, y, core = me // 4, (me // 2) % 2, me % 2

    def at(dz=0, dy=0, dc=0):
        return ((z + dz) % 4) * 4 + ((y + dy) % 2) * 2 + (core + dc) % 2

    z_peers = [(group, at(dz=d)) for d in (1, 2, 3)]
    y_peer = (group, at(dy=1))
    core_peer = (group, at(dc=1))
    x_peer = (1 - group, me)

    own_left = pltpu.make_async_copy(qin_hbm, left.at[0, 0, 0], local_sem.at[0])
    own_right = pltpu.make_async_copy(qout_hbm, right.at[0, 0, 0], local_sem.at[1])
    load_acts = pltpu.make_async_copy(acts_hbm, acts, local_sem.at[2])
    load_grads = pltpu.make_async_copy(grads_hbm, grads, local_sem.at[3])
    own_left.start()
    own_right.start()
    load_acts.start()
    load_grads.start()

    barrier = pltpu.get_barrier_semaphore()
    others = [(group, (me + d) % 16) for d in range(1, 16)]
    for other in others + [x_peer]:
        pl.semaphore_signal(barrier, inc=1, device_id=other, device_id_type=MESH)
    pl.semaphore_wait(barrier, 16)
    own_left.wait()
    own_right.wait()

    sides = (left, right)
    acc_left[...] = jnp.zeros_like(acc_left)
    acc_right[...] = jnp.zeros_like(acc_right)
    next_id = [0]
    sent = []

    def send(src, dst, peer):
        k = next_id[0]
        next_id[0] += 1
        copy = pltpu.make_async_remote_copy(
            src_ref=src, dst_ref=dst, send_sem=send_sem.at[k], recv_sem=recv_sem.at[k],
            device_id=peer, device_id_type=MESH,
        )
        return copy

    steps = []
    for kind, side, start, width in plan:
        buf = sides[side]
        step = dict(kind=kind, side=side, start=start, width=width)
        if kind == "pair":
            mine = pl.ds(pl.multiple_of(start + group * width, 128), width)
            theirs = pl.ds(pl.multiple_of(start + (1 - group) * width, 128), width)
        else:
            mine = pl.ds(start, width)
            theirs = None
        step["z"] = [
            send(buf.at[0, 0, 0, :, mine], buf.at[0, 0, 4 - d, :, mine], z_peers[d - 1])
            for d in (1, 2, 3)
        ]
        step["y0"] = send(buf.at[0, 0, 0, :, mine], buf.at[0, 1, 0, :, mine], y_peer)
        step["y"] = send(buf.at[0, 0, 1:4, :, mine], buf.at[0, 1, 1:4, :, mine], y_peer)
        step["c0"] = send(buf.at[0, 0, :, :, mine], buf.at[1, 0, :, :, mine], core_peer)
        step["c1"] = send(buf.at[0, 1, :, :, mine], buf.at[1, 1, :, :, mine], core_peer)
        if kind == "pair":
            step["x0"] = send(buf.at[0, 0, 1:4, :, mine], buf.at[0, 0, 1:4, :, mine], x_peer)
            step["x1"] = send(buf.at[0, 1, :, :, mine], buf.at[0, 1, :, :, mine], x_peer)
            step["x0r"] = buf.at[0, 0, 1:4, :, theirs]
            step["x1r"] = buf.at[0, 1, :, :, theirs]
            step["d0"] = send(buf.at[0, 0, :, :, theirs], buf.at[1, 0, :, :, theirs], core_peer)
            step["d1"] = send(buf.at[0, 1, :, :, theirs], buf.at[1, 1, :, :, theirs], core_peer)
        steps.append(step)

    def go(copy):
        copy.start()
        sent.append(copy)

    def bring(step):
        for copy in step["z"]:
            go(copy)

    def stage1(step):
        for copy in step["z"]:
            copy.wait_recv()
        go(step["y"])
        if step["kind"] == "pair":
            go(step["x0"])
        go(step["c0"])

    def stage2(step):
        step["y0"].wait_recv()
        step["y"].wait_recv()
        if step["kind"] == "pair":
            go(step["x1"])
        go(step["c1"])

    def stage3a(step):
        step["x0"].wait_recv()
        go(step["d0"])

    def stage3b(step):
        step["x1"].wait_recv()
        go(step["d1"])

    loaded = [False, False]
    pieces = []

    def stage4(step):
        step["c0"].wait_recv()
        step["c1"].wait_recv()
        if step["kind"] == "pair":
            step["d0"].wait_recv()
            step["d1"].wait_recv()
        side, start = step["side"], step["start"]
        if not loaded[side]:
            (load_acts, load_grads)[side].wait()
            loaded[side] = True
        width = step["width"] * (2 if step["kind"] == "pair" else 1)
        for piece in range(start, start + width, 2048):
            pieces.append((side, piece, 2048))

    def multiply():
        side, start, width = pieces.pop(0)
        rows = sides[side][:, :, :, :, start:start + width].reshape(128, width)
        tokens = (acts, grads)[side][:, start:start + width]
        acc = (acc_left, acc_right)[side]
        acc[...] += lax.dot_general(
            rows, tokens, (((1,), (1,)), ((), ())), preferred_element_type=jnp.float32
        )

    for step in steps[:AHEAD]:
        bring(step)
    for step in steps:
        go(step["y0"])
    brought = AHEAD
    stages = dict(z=stage1, y=stage2, x0=stage3a, x1=stage3b, done=stage4)
    for _, i, name in make_order(plan):
        stages[name](steps[i])
        if name == "z" and brought < len(steps):
            bring(steps[brought])
            brought += 1
        if pieces:
            multiply()
    while pieces:
        multiply()

    product = acc_left[...] * acc_right[...]
    tokens = product.shape[1]
    product = product.reshape(4, 4, 8, tokens)
    by_query = product[0] + product[1] + product[2] + product[3]
    row = lax.broadcasted_iota(jnp.int32, (8, 128), 0)
    lane = lax.broadcasted_iota(jnp.int32, (8, 128), 1)
    scores = jnp.zeros((8, 128), jnp.float32)
    for n in range(2):
        valid = lax.broadcasted_iota(jnp.int32, (8, seq_len), 1) < lengths_ref[n]
        for d in range(4):
            part = jnp.where(valid, by_query[d, :, n * seq_len:(n + 1) * seq_len], 0.0)
            total = jnp.sum(jnp.sum(part, axis=0, keepdims=True), axis=1, keepdims=True)
            scores += jnp.where((row == n) & (lane == (z + d) % 4), total, 0.0)

    squares[0] = scores * scores
    spreads = []
    for d in range(1, 16):
        copy = pltpu.make_async_remote_copy(
            src_ref=squares.at[0], dst_ref=squares.at[d], send_sem=sq_send.at[d - 1],
            recv_sem=sq_recv.at[d - 1], device_id=others[d - 1], device_id_type=MESH,
        )
        copy.start()
        spreads.append(copy)
    for copy in sent:
        copy.wait_send()
    for copy in spreads:
        copy.wait_recv()
    total = jnp.sum(jnp.sum(squares[...], axis=0), axis=0, keepdims=True)
    spread = total / 32.0
    out_ref[...] = scores / jnp.sqrt(spread + 1e-06)
    for copy in spreads:
        copy.wait_send()


def kernel_body(train_acts, train_grads, lengths, query_in, query_out):
    tokens, left_cols = train_acts.shape
    right_cols = train_grads.shape[1]
    seq_len = tokens // lengths.shape[0]
    plan = make_plan(left_cols, right_cols)
    copies = count_copies(plan)
    anywhere = pl.BlockSpec(memory_space=pl.ANY)
    tile = pl.pallas_call(
        functools.partial(kernel, plan, seq_len),
        out_shape=jax.ShapeDtypeStruct((8, 128), jnp.float32),
        in_specs=[pl.BlockSpec(memory_space=pltpu.SMEM)] + [anywhere] * 4,
        out_specs=pl.BlockSpec(memory_space=pltpu.VMEM),
        scratch_shapes=[
            pltpu.VMEM((tokens, left_cols), jnp.bfloat16),
            pltpu.VMEM((tokens, right_cols), jnp.bfloat16),
            pltpu.VMEM((2, 2, 4, 8, left_cols), jnp.bfloat16),
            pltpu.VMEM((2, 2, 4, 8, right_cols), jnp.bfloat16),
            pltpu.VMEM((128, tokens), jnp.float32),
            pltpu.VMEM((128, tokens), jnp.float32),
            pltpu.VMEM((16, 8, 128), jnp.float32),
            pltpu.SemaphoreType.DMA((4,)),
            pltpu.SemaphoreType.DMA((copies,)),
            pltpu.SemaphoreType.DMA((copies,)),
            pltpu.SemaphoreType.DMA((15,)),
            pltpu.SemaphoreType.DMA((15,)),
        ],
        compiler_params=pltpu.CompilerParams(
            collective_id=0, has_side_effects=True, vmem_limit_bytes=56 * 2**20
        ),
        cost_estimate=pl.CostEstimate(
            flops=2 * 128 * tokens * (left_cols + right_cols),
            bytes_accessed=2 * tokens * (left_cols + right_cols),
            transcendentals=0,
        ),
    )(lengths, train_acts, train_grads, query_in, query_out)
    return tile[:2, :4]


def solution(mesh):
    in_specs = (
        P(("groups", "dp"), None),
        P(("groups", "dp"), None),
        P(("groups", "dp")),
        P("dp", None),
        P("dp", None),
    )
    out_specs = P(("groups", "dp"), None)
    here = mesh.shape["groups"] == 2 and mesh.shape["dp"] == 16
    return jax.shard_map(
        kernel_body if here else plain_body,
        mesh=mesh, in_specs=in_specs, out_specs=out_specs, check_vma=False,
    )
```

```python
import functools

import jax
import jax.numpy as jnp
from jax import lax
from jax.experimental import pallas as pl
from jax.experimental.pallas import tpu as pltpu
from jax.sharding import PartitionSpec as P

RANK = 32
MESH = pl.DeviceIdType.MESH
LEFT_PAIRS = (2048, 2048)
RIGHT_PAIRS = (2048, 1024)
BOTH = (2048, 2048, 2048, 1024, 1024)
AHEAD = 2
LATENCY = 3.0


def plain_body(train_acts, train_grads, lengths, query_in, query_out):
    token_rows = train_acts.shape[0]
    seq_count = lengths.shape[0]
    seq_len = token_rows // seq_count
    device_count = lax.axis_size("dp")
    total_rows = query_in.shape[0] * device_count
    query_count = total_rows // RANK
    valid_mask = (jnp.arange(seq_len, dtype=jnp.int32)[None, :] < lengths[:, None]).astype(
        jnp.float32
    )
    all_left, all_right = (
        lax.all_gather(query_in, "dp", axis=0, tiled=True),
        lax.all_gather(query_out, "dp", axis=0, tiled=True),
    )
    left_proj = lax.dot_general(
        all_left, train_acts, (((1,), (1,)), ((), ())), preferred_element_type=jnp.float32
    )
    right_proj = lax.dot_general(
        all_right, train_grads, (((1,), (1,)), ((), ())), preferred_element_type=jnp.float32
    )
    product = (left_proj * right_proj).reshape(all_left.shape[0], seq_count, seq_len)
    onehot = (
        (jnp.arange(total_rows, dtype=jnp.int32) // RANK)[None, :]
        == jnp.arange(query_count, dtype=jnp.int32)[:, None]
    ).astype(jnp.float32)
    scores = jnp.dot(
        onehot, jnp.sum(product * valid_mask[None], axis=2), precision=lax.Precision.HIGHEST
    )
    squares = lax.psum(jnp.sum(scores * scores, axis=1), "dp")
    spread = squares / (seq_count * device_count)
    return (scores / jnp.sqrt(spread + 1e-06)[:, None]).T


def make_plan(left_cols, right_cols):
    plan = []

    def add(kind, side, start, count, widths):
        for k in range(len(widths)):
            width = widths[k]
            plan.append((kind, side, start, width))
            start += width * (2 if kind == "pair" else 1)
            count -= width * (2 if kind == "pair" else 1)
        assert count == 0
        return start

    add("pair", 0, 0, left_cols, LEFT_PAIRS)
    start = add("pair", 1, 0, 2 * sum(RIGHT_PAIRS), RIGHT_PAIRS)
    add("both", 1, start, right_cols - start, BOTH)
    return plan


def make_order(plan):
    events, asks = [], []
    z_free = y_free = x_free = 0.0
    ready = []
    for i, (kind, _, _, width) in enumerate(plan):
        block = width / 2048
        z_free += 4.0 * block
        z_in = z_free + LATENCY
        y_free = max(y_free, z_in) + 3.0 * block
        y_in = y_free + LATENCY
        events += [(z_in, i, "z"), (y_in, i, "y")]
        ready.append(y_in)
        if kind == "pair":
            asks += [(z_in, i, "x0", 3.0 * block), (y_in, i, "x1", 4.0 * block)]
    for time, i, name, blocks in sorted(asks):
        x_free = max(x_free, time) + blocks
        events.append((x_free + LATENCY, i, name))
        ready[i] = max(ready[i], x_free + LATENCY)
    for i, time in enumerate(ready):
        events.append((time + LATENCY, i, "done"))
    return sorted(events)


def count_copies(plan):
    return sum(11 if step[0] == "pair" else 7 for step in plan)


def kernel(
    plan, seq_len, lengths_ref, acts_hbm, grads_hbm, qin_hbm, qout_hbm, out_ref,
    acts, grads, left, right, acc_left, acc_right, squares, local_sem, send_sem, recv_sem,
    sq_send, sq_recv,
):
    group = lax.axis_index("groups")
    me = lax.axis_index("dp")
    z, y, core = me // 4, (me // 2) % 2, me % 2

    def at(dz=0, dy=0, dc=0):
        return ((z + dz) % 4) * 4 + ((y + dy) % 2) * 2 + (core + dc) % 2

    z_peers = [(group, at(dz=d)) for d in (1, 2, 3)]
    y_peer = (group, at(dy=1))
    core_peer = (group, at(dc=1))
    x_peer = (1 - group, me)

    own_left = pltpu.make_async_copy(qin_hbm, left.at[0, 0, 0], local_sem.at[0])
    own_right = pltpu.make_async_copy(qout_hbm, right.at[0, 0, 0], local_sem.at[1])
    load_acts = pltpu.make_async_copy(acts_hbm, acts, local_sem.at[2])
    load_grads = pltpu.make_async_copy(grads_hbm, grads, local_sem.at[3])
    own_left.start()
    own_right.start()
    load_acts.start()
    load_grads.start()

    barrier = pltpu.get_barrier_semaphore()
    others = [(group, (me + d) % 16) for d in range(1, 16)]
    for other in others + [x_peer]:
        pl.semaphore_signal(barrier, inc=1, device_id=other, device_id_type=MESH)
    pl.semaphore_wait(barrier, 16)
    own_left.wait()
    own_right.wait()

    sides = (left, right)
    acc_left[...] = jnp.zeros_like(acc_left)
    acc_right[...] = jnp.zeros_like(acc_right)
    next_id = [0]
    sent = []

    def send(src, dst, peer):
        k = next_id[0]
        next_id[0] += 1
        copy = pltpu.make_async_remote_copy(
            src_ref=src, dst_ref=dst, send_sem=send_sem.at[k], recv_sem=recv_sem.at[k],
            device_id=peer, device_id_type=MESH,
        )
        return copy

    steps = []
    for kind, side, start, width in plan:
        buf = sides[side]
        step = dict(kind=kind, side=side, start=start, width=width)
        if kind == "pair":
            mine = pl.ds(pl.multiple_of(start + group * width, 128), width)
            theirs = pl.ds(pl.multiple_of(start + (1 - group) * width, 128), width)
        else:
            mine = pl.ds(start, width)
            theirs = None
        step["z"] = [
            send(buf.at[0, 0, 0, :, mine], buf.at[0, 0, 4 - d, :, mine], z_peers[d - 1])
            for d in (1, 2, 3)
        ]
        step["y0"] = send(buf.at[0, 0, 0, :, mine], buf.at[0, 1, 0, :, mine], y_peer)
        step["y"] = send(buf.at[0, 0, 1:4, :, mine], buf.at[0, 1, 1:4, :, mine], y_peer)
        step["c0"] = send(buf.at[0, 0, :, :, mine], buf.at[1, 0, :, :, mine], core_peer)
        step["c1"] = send(buf.at[0, 1, :, :, mine], buf.at[1, 1, :, :, mine], core_peer)
        if kind == "pair":
            step["x0"] = send(buf.at[0, 0, 1:4, :, mine], buf.at[0, 0, 1:4, :, mine], x_peer)
            step["x1"] = send(buf.at[0, 1, :, :, mine], buf.at[0, 1, :, :, mine], x_peer)
            step["x0r"] = buf.at[0, 0, 1:4, :, theirs]
            step["x1r"] = buf.at[0, 1, :, :, theirs]
            step["d0"] = send(buf.at[0, 0, :, :, theirs], buf.at[1, 0, :, :, theirs], core_peer)
            step["d1"] = send(buf.at[0, 1, :, :, theirs], buf.at[1, 1, :, :, theirs], core_peer)
        steps.append(step)

    def go(copy):
        copy.start()
        sent.append(copy)

    def bring(step):
        for copy in step["z"]:
            go(copy)

    def stage1(step):
        for copy in step["z"]:
            copy.wait_recv()
        go(step["y"])
        if step["kind"] == "pair":
            go(step["x0"])
        go(step["c0"])

    def stage2(step):
        step["y0"].wait_recv()
        step["y"].wait_recv()
        if step["kind"] == "pair":
            go(step["x1"])
        go(step["c1"])

    def stage3a(step):
        step["x0"].wait_recv()
        go(step["d0"])

    def stage3b(step):
        step["x1"].wait_recv()
        go(step["d1"])

    loaded = [False, False]
    pieces = []

    def stage4(step):
        step["c0"].wait_recv()
        step["c1"].wait_recv()
        if step["kind"] == "pair":
            step["d0"].wait_recv()
            step["d1"].wait_recv()
        side, start = step["side"], step["start"]
        if not loaded[side]:
            (load_acts, load_grads)[side].wait()
            loaded[side] = True
        width = step["width"] * (2 if step["kind"] == "pair" else 1)
        for piece in range(start, start + width, 2048):
            pieces.append((side, piece, min(2048, width)))

    def multiply():
        side, start, width = pieces.pop(0)
        rows = sides[side][:, :, :, :, start:start + width].reshape(128, width)
        tokens = (acts, grads)[side][:, start:start + width]
        acc = (acc_left, acc_right)[side]
        acc[...] += lax.dot_general(
            rows, tokens, (((1,), (1,)), ((), ())), preferred_element_type=jnp.float32
        )

    for step in steps[:AHEAD]:
        bring(step)
    for step in steps:
        go(step["y0"])
    brought = AHEAD
    stages = dict(z=stage1, y=stage2, x0=stage3a, x1=stage3b, done=stage4)
    for _, i, name in make_order(plan):
        stages[name](steps[i])
        if name == "z" and brought < len(steps):
            bring(steps[brought])
            brought += 1
        if pieces:
            multiply()
    while pieces:
        multiply()

    product = acc_left[...] * acc_right[...]
    tokens = product.shape[1]
    product = product.reshape(4, 4, 8, tokens)
    by_query = product[0] + product[1] + product[2] + product[3]
    row = lax.broadcasted_iota(jnp.int32, (8, 128), 0)
    lane = lax.broadcasted_iota(jnp.int32, (8, 128), 1)
    scores = jnp.zeros((8, 128), jnp.float32)
    for n in range(2):
        valid = lax.broadcasted_iota(jnp.int32, (8, seq_len), 1) < lengths_ref[n]
        for d in range(4):
            part = jnp.where(valid, by_query[d, :, n * seq_len:(n + 1) * seq_len], 0.0)
            total = jnp.sum(jnp.sum(part, axis=0, keepdims=True), axis=1, keepdims=True)
            scores += jnp.where((row == n) & (lane == (z + d) % 4), total, 0.0)

    squares[0] = scores * scores
    spreads = []
    for d in range(1, 16):
        copy = pltpu.make_async_remote_copy(
            src_ref=squares.at[0], dst_ref=squares.at[d], send_sem=sq_send.at[d - 1],
            recv_sem=sq_recv.at[d - 1], device_id=others[d - 1], device_id_type=MESH,
        )
        copy.start()
        spreads.append(copy)
    for copy in sent:
        copy.wait_send()
    for copy in spreads:
        copy.wait_recv()
    total = jnp.sum(jnp.sum(squares[...], axis=0), axis=0, keepdims=True)
    spread = total / 32.0
    out_ref[...] = scores / jnp.sqrt(spread + 1e-06)
    for copy in spreads:
        copy.wait_send()


def kernel_body(train_acts, train_grads, lengths, query_in, query_out):
    tokens, left_cols = train_acts.shape
    right_cols = train_grads.shape[1]
    seq_len = tokens // lengths.shape[0]
    plan = make_plan(left_cols, right_cols)
    copies = count_copies(plan)
    anywhere = pl.BlockSpec(memory_space=pl.ANY)
    tile = pl.pallas_call(
        functools.partial(kernel, plan, seq_len),
        out_shape=jax.ShapeDtypeStruct((8, 128), jnp.float32),
        in_specs=[pl.BlockSpec(memory_space=pltpu.SMEM)] + [anywhere] * 4,
        out_specs=pl.BlockSpec(memory_space=pltpu.VMEM),
        scratch_shapes=[
            pltpu.VMEM((tokens, left_cols), jnp.bfloat16),
            pltpu.VMEM((tokens, right_cols), jnp.bfloat16),
            pltpu.VMEM((2, 2, 4, 8, left_cols), jnp.bfloat16),
            pltpu.VMEM((2, 2, 4, 8, right_cols), jnp.bfloat16),
            pltpu.VMEM((128, tokens), jnp.float32),
            pltpu.VMEM((128, tokens), jnp.float32),
            pltpu.VMEM((16, 8, 128), jnp.float32),
            pltpu.SemaphoreType.DMA((4,)),
            pltpu.SemaphoreType.DMA((copies,)),
            pltpu.SemaphoreType.DMA((copies,)),
            pltpu.SemaphoreType.DMA((15,)),
            pltpu.SemaphoreType.DMA((15,)),
        ],
        compiler_params=pltpu.CompilerParams(
            collective_id=0, has_side_effects=True, vmem_limit_bytes=56 * 2**20
        ),
        cost_estimate=pl.CostEstimate(
            flops=2 * 128 * tokens * (left_cols + right_cols),
            bytes_accessed=2 * tokens * (left_cols + right_cols),
            transcendentals=0,
        ),
    )(lengths, train_acts, train_grads, query_in, query_out)
    return tile[:2, :4]


def solution(mesh):
    in_specs = (
        P(("groups", "dp"), None),
        P(("groups", "dp"), None),
        P(("groups", "dp")),
        P("dp", None),
        P("dp", None),
    )
    out_specs = P(("groups", "dp"), None)
    here = mesh.shape["groups"] == 2 and mesh.shape["dp"] == 16
    return jax.shard_map(
        kernel_body if here else plain_body,
        mesh=mesh, in_specs=in_specs, out_specs=out_specs, check_vma=False,
    )
```
